512 devices in a mesh: blk: 64 (over z_lo, x, core), rep: 8 (over y, z_hi).
Axes of the slice: x: 4, y: 4, z: 16 (z_hi: 2, z_lo: 8; z = z_hi * 8 + z_lo), core: 2. Of those that a mesh axis runs over, the one named last changes fastest.
Arguments:
- features: bfloat16 [32768, 128], P('blk'), may hold values from -6 to 6
- adjacency: bfloat16 [64, 8, 6, 512, 512], P('blk', 'rep'), may hold values from -0.0390625 to 0.0390625
- tile_column: int32 [64, 8, 6], P('blk', 'rep'), may hold values from -1 to 63, as said below
- weight: bfloat16 [128, 128], replicated, may hold values from -0.5 to 0.5
- out_bias: bfloat16 [128], replicated, may hold values from -3 to 3
Outputs:
- output: bfloat16 [32768, 128], P(('blk', 'rep'))
The draws below stay inside these ranges and needn't reach their ends.
Inputs may be any that keep to these rules, and one draw needn't show every extreme that they name: `tile_column`: for row block b and replica r, each live slot holds a column block (b - r - 8 * t) mod 64 with t in 0 to 7; live columns of one device are distinct; live slots come first; each device has one or more live slots; some device has all 6 live.
All inputs are finite; a program needn't handle non-finite values.
Results may differ from the reference program's by a relative error of at most 0.0043.
Values may be sent and summed in bfloat16 or wider, within the bound.
No kernel may reach another device: no remote copies, remote signals or barrier semaphores. Data moves between devices by JAX's collectives and lax.ppermute only.
A program may use at most 64 MiB of HBM per device.

```python
import jax
import jax.numpy as jnp
from jax import lax

F = 128
R = 512
TILES_DEV = 6
BLOCKS = 64
REPS = 8
NODES = 32768
N_REP = 8


def draw_tile_column(key, part):
    key = jax.random.fold_in(key, 7)
    section_count = BLOCKS // REPS
    key_count, key_order = jax.random.split(key)
    counts = jax.random.randint(key_count, (BLOCKS, REPS), 1, TILES_DEV + 1)
    counts = counts.at[0, 0].set(TILES_DEV)
    scores = jax.random.randint(key_order, (BLOCKS, REPS, section_count), 0, 1 << 20) * section_count
    scores = scores + jnp.arange(section_count, dtype=jnp.int32)[None, None, :]
    picked = jnp.argsort(scores, axis=-1, stable=True)[:, :, :TILES_DEV].astype(jnp.int32)
    row_ids = jnp.arange(BLOCKS, dtype=jnp.int32)[:, None, None]
    rep_ids = jnp.arange(REPS, dtype=jnp.int32)[None, :, None]
    column = jnp.mod(row_ids - rep_ids - REPS * picked, BLOCKS)
    is_live = jnp.arange(TILES_DEV, dtype=jnp.int32)[None, None, :] < counts[:, :, None]
    return jnp.where(is_live, column, -1).astype(jnp.int32)


def steps_of(key, dims, cuts, least, high):
    gain, own = 1.0, jax.random.fold_in(key, 6)
    for axis_at, shards_of in cuts:
        draws = jnp.exp(jax.random.uniform(jax.random.fold_in(own, axis_at), (shards_of,), jnp.float32, least / len(cuts), high / len(cuts)))
        gain = gain * jnp.repeat(draws, dims[axis_at] // shards_of).reshape([-1 if axis == axis_at else 1 for axis in range(len(dims))])
    return gain


def bell_draw(key, extent, deviation, reach, pieces=(), held_as=jnp.bfloat16):
    entries = deviation * jax.random.normal(key, extent, jnp.float32)
    if pieces:
        entries = entries * steps_of(key, extent, pieces, -0.22, 0.18)
    return jnp.clip(entries, -reach, reach).astype(held_as)


def setup_inputs(seed: int = 0) -> dict:
    streams_of = jax.random.split(jax.random.key(seed), 6)
    return {
        "features": bell_draw(streams_of[0], (NODES, F), 1.0, 6.0, ((0, 64),)),
        "adjacency": bell_draw(streams_of[1], (BLOCKS, REPS, TILES_DEV, R, R), (R * TILES_DEV * N_REP) ** -0.5, 0.0390625, ((0, 64), (1, 8))),
        "tile_column": draw_tile_column(jax.random.fold_in(streams_of[5], 71), 0),
        "weight": bell_draw(streams_of[3], (F, F), F ** -0.5, 0.5),
        "out_bias": bell_draw(streams_of[4], (F,), 0.5, 3.0),
    }


def reference(features, adjacency, tile_column, weight, out_bias):
    node_blocks = features.reshape(BLOCKS, R, F)

    def block_sum(row_block):
        columns = lax.dynamic_index_in_dim(tile_column, row_block, 0, False)
        is_live = columns >= 0
        safe_columns = jnp.maximum(columns, 0).astype(jnp.int32)
        selected = node_blocks[safe_columns].astype(jnp.float32)
        tile_values = lax.dynamic_index_in_dim(adjacency, row_block, 0, False).astype(jnp.float32)
        products = jnp.einsum("rkij,rkjf->rkif", tile_values, selected)
        return jnp.sum(jnp.where(is_live[:, :, None, None], products, 0.0), axis=(0, 1))

    aggregate = lax.map(block_sum, jnp.arange(BLOCKS, dtype=jnp.int32))
    hidden = aggregate.reshape(BLOCKS * R, F).astype(jnp.bfloat16)
    result = jnp.dot(hidden, weight, preferred_element_type=jnp.float32) + out_bias.astype(jnp.float32)
    return jnp.maximum(result, 0.0).astype(jnp.bfloat16)
```

```python
import functools

import jax
import jax.numpy as jnp
from jax import lax
from jax.experimental import pallas as pl
from jax.experimental.pallas import tpu as pltpu
from jax.sharding import PartitionSpec as P

SIDE, RING, LINE = 4, 16, 8


def device(x, y, z, core):
    x, y, z = x % SIDE, y % SIDE, z % RING
    return ((z % LINE * SIDE + x) * 2 + core) * LINE + y * 2 + z // LINE


def members(diagonal, half, core):
    kind = (2 * diagonal + core - half) % LINE
    by_hops = (1, 0, 2, 3) if half == 1 and core == 0 else (2, 1, 3, 0)
    return kind, by_hops


@functools.cache
def plan():
    groups, wanted = [], {}
    for low in range(0, RING, 2):
        half = low // LINE
        for diagonal in range(SIDE):
            for core in range(2):
                kind, by_hops = members(diagonal, half, core)
                group = []
                for offset in range(-3, 5):
                    z, hops = (low, -offset) if offset <= 0 else (low + 1, offset - 1)
                    y = by_hops[hops]
                    member = device(diagonal + y, y, z, core)
                    group.append(member)
                    wanted.setdefault(((low + offset) % RING, kind), []).append((y, member))
                groups.append(group)
    pairs = []
    for (z, kind), receivers in wanted.items():
        free = set(range(SIDE))
        for exact in (True, False):
            for y, member in receivers:
                if exact and y in free:
                    pass
                elif not exact and member not in placed:
                    y = min(free, key=lambda other: min((other - y) % SIDE, (y - other) % SIDE))
                else:
                    continue
                if exact:
                    placed = {m for _, m in pairs}
                free.discard(y)
                pairs.append((device(kind // 2, y, z, kind % 2), member))
            placed = {m for _, m in pairs}
    return groups, pairs


def aggregate_kernel(slots, order, adjacency, blocks, out, total):
    total[...] = jnp.zeros_like(total)
    for slot in range(adjacency.shape[0]):

        @pl.when(slots[slot] >= 0)
        def _():
            total[...] += jnp.dot(
                adjacency[slot], blocks[order[slot]], preferred_element_type=jnp.float32
            )

    out[...] = total[...].astype(out.dtype)


def project_kernel(parts, weight, bias, out):
    hidden = jnp.sum(parts[...].astype(jnp.float32), axis=0).astype(jnp.bfloat16)
    result = jnp.dot(hidden, weight[...], preferred_element_type=jnp.float32)
    out[...] = jnp.maximum(result + bias[...].astype(jnp.float32), 0.0).astype(out.dtype)


def local(features, adjacency, tile_column, weight, out_bias):
    groups, pairs = plan()
    axes = ("blk", "rep")
    rows, width = features.shape
    tiles = adjacency.reshape(adjacency.shape[2:])
    columns = tile_column.reshape(-1)
    low = lax.axis_index("blk") // LINE & ~1
    order = (columns // LINE - low + 3) & (LINE - 1)

    first = lax.ppermute(features, axes, pairs)
    blocks = lax.all_to_all(
        jnp.broadcast_to(first[None], (LINE, rows, width)), axes, 0, 0, axis_index_groups=groups
    )
    vmem, smem = pl.BlockSpec(memory_space=pltpu.VMEM), pl.BlockSpec(memory_space=pltpu.SMEM)
    partial = pl.pallas_call(
        aggregate_kernel,
        out_shape=jax.ShapeDtypeStruct((rows, width), jnp.bfloat16),
        in_specs=[smem, smem, vmem, vmem],
        out_specs=vmem,
        scratch_shapes=[pltpu.VMEM((rows, width), jnp.float32)],
        compiler_params=pltpu.CompilerParams(vmem_limit_bytes=16 * 2**20),
    )(columns, order, tiles, blocks)
    replicas = lax.axis_size("rep")
    parts = lax.all_to_all(partial.reshape(replicas, rows // replicas, width), "rep", 0, 0)
    return pl.pallas_call(
        project_kernel,
        out_shape=jax.ShapeDtypeStruct((rows // replicas, width), jnp.bfloat16),
        in_specs=[vmem, vmem, vmem],
        out_specs=vmem,
    )(parts, weight, out_bias.reshape(1, width))


def solution(mesh):
    in_specs = (P("blk", None), P("blk", "rep", None, None, None), P("blk", "rep", None), P(), P())
    out_specs = P(("blk", "rep"), None)
    return jax.shard_map(local, mesh=mesh, in_specs=in_specs, out_specs=out_specs, check_vma=False)
```

```python
import functools
import itertools

import jax
import jax.numpy as jnp
from jax import lax
from jax.experimental import pallas as pl
from jax.experimental.pallas import tpu as pltpu
from jax.sharding import PartitionSpec as P

SIDE, RING, LINE = 4, 16, 8
BY_HOPS = (2, 1, 3, 0), (1, 0, 2, 3)
REDUCE_ORDER = 1, 3, 5, 7, 0, 2, 4, 6


def device(x, y, z, core):
    x, y, z = x % SIDE, y % SIDE, z % RING
    return ((z % LINE * SIDE + x) * 2 + core) * LINE + y * 2 + z // LINE


def apart(one, other, size):
    return min((one - other) % size, (other - one) % size)


@functools.cache
def plan():
    groups, receivers = [], {}
    for low in range(0, RING, 2):
        half = low // LINE
        for diagonal, core in itertools.product(range(SIDE), range(2)):
            kind = (2 * diagonal + core - half) % LINE
            by_hops = BY_HOPS[half == 1 and core == 0]
            group = []
            for later, at in itertools.product(range(2), range(SIDE)):
                hops = (at - 1) % SIDE
                y = by_hops[hops]
                place = ((diagonal + y) % SIDE, y, low + later, core)
                group.append(device(*place))
                key = (low + later + (hops if later else -hops)) % RING, kind
                receivers.setdefault(key, []).append(place)
            groups.append(group)
    pairs = []
    for (z, kind), places in receivers.items():

        def cost(rows):
            hops = [
                apart(kind // 2, place[0], SIDE) + apart(row, place[1], SIDE) + apart(z, place[2], RING)
                for row, place in zip(rows, places)
            ]
            return max(hops), sum(hops)

        rows = min(itertools.permutations(range(SIDE)), key=cost)
        pairs += [
            (device(kind // 2, row, z, kind % 2), device(*place)) for row, place in zip(rows, places)
        ]
    return groups, pairs


def aggregate_kernel(columns, adjacency, blocks, out, total):
    low = lax.axis_index("blk") // LINE & ~1
    slots = range(adjacency.shape[0])
    total[...] = jnp.zeros_like(total)
    for slot in slots:

        @pl.when(columns[slot] >= 0)
        def _():
            ahead = (columns[slot] // LINE - low + 3) & (LINE - 1)
            hops = jnp.where(ahead > 3, ahead - 4, 3 - ahead)
            place = (ahead & 4) + ((hops + 1) & 3)
            total[...] += jnp.dot(adjacency[slot], blocks[place], preferred_element_type=jnp.float32)

    own = out.shape[1]
    for at, replica in enumerate(REDUCE_ORDER):
        out[at] = total[replica * own : (replica + 1) * own].astype(out.dtype)


def project_kernel(parts, weight, bias, out):
    hidden = jnp.sum(parts[...].astype(jnp.float32), axis=0).astype(jnp.bfloat16)
    result = jnp.dot(hidden, weight[...], preferred_element_type=jnp.float32)
    out[...] = jnp.maximum(result + bias[...].astype(jnp.float32), 0.0).astype(out.dtype)


def local(features, adjacency, tile_column, weight, out_bias):
    groups, pairs = plan()
    axes = ("blk", "rep")
    rows, width = features.shape
    replicas = lax.axis_size("rep")

    first = lax.ppermute(features, axes, pairs)
    blocks = lax.all_to_all(
        jnp.broadcast_to(first[None], (LINE, rows, width)), axes, 0, 0, axis_index_groups=groups
    )
    vmem, smem = pl.BlockSpec(memory_space=pltpu.VMEM), pl.BlockSpec(memory_space=pltpu.SMEM)
    partial = pl.pallas_call(
        aggregate_kernel,
        out_shape=jax.ShapeDtypeStruct((replicas, rows // replicas, width), jnp.bfloat16),
        in_specs=[smem, vmem, vmem],
        out_specs=vmem,
        scratch_shapes=[
            pltpu.VMEM((rows, width), jnp.float32),
        ],
        compiler_params=pltpu.CompilerParams(vmem_limit_bytes=8 * 2**20),
    )(tile_column.reshape(-1), adjacency.reshape(adjacency.shape[2:]), blocks)
    parts = lax.all_to_all(partial, "rep", 0, 0, axis_index_groups=[list(REDUCE_ORDER)])
    return pl.pallas_call(
        project_kernel,
        out_shape=jax.ShapeDtypeStruct((rows // replicas, width), jnp.bfloat16),
        in_specs=[vmem, vmem, vmem],
        out_specs=vmem,
        compiler_params=pltpu.CompilerParams(vmem_limit_bytes=4 * 2**20),
    )(parts, weight, out_bias.reshape(1, width))


def solution(mesh):
    in_specs = (P("blk", None), P("blk", "rep", None, None, None), P("blk", "rep", None), P(), P())
    out_specs = P(("blk", "rep"), None)
    return jax.shard_map(local, mesh=mesh, in_specs=in_specs, out_specs=out_specs, check_vma=False)
```

```python
import functools
import itertools

import jax
import jax.numpy as jnp
from jax import lax
from jax.experimental import pallas as pl
from jax.experimental.pallas import tpu as pltpu
from jax.sharding import PartitionSpec as P

SIDE, RING, LINE = 4, 16, 8
REDUCE_ORDER = 1, 3, 5, 7, 0, 2, 4, 6


def device(x, y, z, core):
    x, y, z = x % SIDE, y % SIDE, z % RING
    return ((z % LINE * SIDE + x) * 2 + core) * LINE + y * 2 + z // LINE


def user(kind, y, z):
    half = z % RING // LINE
    core = (kind + half) % 2
    return ((kind - core + half) // 2 + y) % SIDE, y, z % RING, core


def apart(one, other, size):
    return min((one - other) % size, (other - one) % size)


@functools.cache
def plan():
    groups, receivers = [], ({}, {})
    for kind in range(LINE):
        even = 1 - kind % 2
        for low, first in itertools.product(range(even, RING, 2), (even, even + 2)):
            group = []
            for z in (low, low + 1):
                pair = [user(kind, (first + i) % SIDE, z) for i in range(2)]
                group += sorted(pair, key=lambda place: apart(place[0], kind // 2, SIDE))
            groups.append([device(*place) for place in group])
            for later, at in itertools.product(range(2), range(SIDE)):
                hops = SIDE - 1 - at
                key = (low + later + (hops if later else -hops)) % RING, kind
                receivers[at % 2].setdefault(key, []).append(group[2 * later + at // 2])
    permutes = []
    for wanted in receivers:
        pairs = []
        for (z, kind), places in wanted.items():

            def cost(rows):
                hops = [
                    apart(kind // 2, place[0], SIDE) + apart(row, place[1], SIDE) + apart(z, place[2], RING)
                    for row, place in zip(rows, places)
                ]
                return max(hops), sum(hops)

            rows = min(itertools.permutations(range(SIDE)), key=cost)
            pairs += [
                (device(kind // 2, row, z, kind % 2), device(*place)) for row, place in zip(rows, places)
            ]
        permutes.append(pairs)
    return groups, permutes


def aggregate_kernel(columns, adjacency, blocks, out):
    blk, rep = lax.axis_index("blk"), lax.axis_index("rep")
    low = blk // LINE - ((blk // LINE ^ blk ^ rep ^ 1) & 1)
    slots = range(adjacency.shape[0])
    total = None
    for slot in slots:
        ahead = (columns[slot] // LINE - low + 3) & (LINE - 1)
        block = blocks[jnp.where(ahead > 3, ahead ^ 3, ahead)]
        block = jnp.where(columns[slot] >= 0, block, jnp.zeros_like(block))
        product = jnp.dot(adjacency[slot], block, preferred_element_type=jnp.float32)
        total = product if total is None else total + product

    own = out.shape[1]
    for at, replica in enumerate(REDUCE_ORDER):
        out[at] = total[replica * own : (replica + 1) * own].astype(out.dtype)


def project_kernel(parts, weight, bias, out):
    hidden = jnp.sum(parts[...].astype(jnp.float32), axis=0).astype(jnp.bfloat16)
    result = jnp.dot(hidden, weight[...], preferred_element_type=jnp.float32)
    out[...] = jnp.maximum(result + bias[...].astype(jnp.float32), 0.0).astype(out.dtype)


def local(features, adjacency, tile_column, weight, out_bias):
    groups, permutes = plan()
    axes = ("blk", "rep")
    rows, width = features.shape
    replicas = lax.axis_size("rep")

    held = jnp.stack([lax.ppermute(features, axes, pairs) for pairs in permutes])
    blocks = lax.all_to_all(
        jnp.broadcast_to(held[None], (len(groups[0]),) + held.shape), axes, 0, 0, axis_index_groups=groups
    ).reshape(LINE, rows, width)
    vmem, smem = pl.BlockSpec(memory_space=pltpu.VMEM), pl.BlockSpec(memory_space=pltpu.SMEM)
    partial = pl.pallas_call(
        aggregate_kernel,
        out_shape=jax.ShapeDtypeStruct((replicas, rows // replicas, width), jnp.bfloat16),
        in_specs=[smem, vmem, vmem],
        out_specs=vmem,
        compiler_params=pltpu.CompilerParams(vmem_limit_bytes=8 * 2**20),
    )(tile_column.reshape(-1), adjacency.reshape(adjacency.shape[2:]), blocks)
    parts = lax.all_to_all(partial, "rep", 0, 0, axis_index_groups=[list(REDUCE_ORDER)])
    return pl.pallas_call(
        project_kernel,
        out_shape=jax.ShapeDtypeStruct((rows // replicas, width), jnp.bfloat16),
        in_specs=[vmem, vmem, vmem],
        out_specs=vmem,
        compiler_params=pltpu.CompilerParams(vmem_limit_bytes=4 * 2**20),
    )(parts, weight, out_bias.reshape(1, width))


def solution(mesh):
    in_specs = (P("blk", None), P("blk", "rep", None, None, None), P("blk", "rep", None), P(), P())
    out_specs = P(("blk", "rep"), None)
    return jax.shard_map(local, mesh=mesh, in_specs=in_specs, out_specs=out_specs, check_vma=False)
```

```python
import functools
import itertools

import jax
import jax.numpy as jnp
from jax import lax
from jax.experimental import pallas as pl
from jax.experimental.pallas import tpu as pltpu
from jax.sharding import PartitionSpec as P

SIDE, RING, LINE = 4, 16, 8
REDUCE_ORDER = 1, 0, 3, 2, 5, 4, 7, 6


def device(x, y, z, core):
    x, y, z = x % SIDE, y % SIDE, z % RING
    return ((z % LINE * SIDE + x) * 2 + core) * LINE + y * 2 + z // LINE


def user(kind, y, z):
    half = z % RING // LINE
    core = (kind + half) % 2
    return ((kind - core + half) // 2 + y) % SIDE, y, z % RING, core


def apart(one, other, size):
    return min((one - other) % size, (other - one) % size)


@functools.cache
def plan():
    groups, receivers = [], ({}, {})
    for kind in range(LINE):
        even = 1 - kind % 2
        for low, first in itertools.product(range(even, RING, 2), (even, even + 2)):
            group = []
            for z in (low, low + 1):
                pair = [user(kind, (first + i) % SIDE, z) for i in range(2)]
                group += sorted(pair, key=lambda place: apart(place[0], kind // 2, SIDE))
            groups.append([device(*place) for place in group])
            for later, at in itertools.product(range(2), range(SIDE)):
                hops = SIDE - 1 - at
                key = (low + later + (hops if later else -hops)) % RING, kind
                receivers[at % 2].setdefault(key, []).append(group[2 * later + at // 2])
    permutes = []
    for wanted in receivers:
        pairs = []
        for (z, kind), places in wanted.items():

            def cost(rows):
                hops = [
                    apart(kind // 2, place[0], SIDE) + apart(row, place[1], SIDE) + apart(z, place[2], RING)
                    for row, place in zip(rows, places)
                ]
                return max(hops), sum(hops)

            rows = min(itertools.permutations(range(SIDE)), key=cost)
            pairs += [
                (device(kind // 2, row, z, kind % 2), device(*place)) for row, place in zip(rows, places)
            ]
        permutes.append(pairs)
    return groups, permutes


def aggregate_kernel(columns, adjacency, blocks, out):
    blk, rep = lax.axis_index("blk"), lax.axis_index("rep")
    low = blk // LINE - ((blk // LINE ^ blk ^ rep ^ 1) & 1)
    slots = range(adjacency.shape[0])
    total = None
    for slot in slots:
        ahead = (columns[slot] // LINE - low + 3) & (LINE - 1)
        block = blocks[jnp.where(ahead > 3, ahead ^ 3, ahead)]
        block = jnp.where(columns[slot] >= 0, block, jnp.zeros_like(block))
        product = jnp.dot(adjacency[slot], block, preferred_element_type=jnp.float32)
        total = product if total is None else total + product

    own = out.shape[1]
    for at, replica in enumerate(REDUCE_ORDER):
        out[at] = total[replica * own : (replica + 1) * own].astype(out.dtype)


def project_kernel(parts, weight, bias, out):
    hidden = jnp.sum(parts[...].astype(jnp.float32), axis=0).astype(jnp.bfloat16)
    result = jnp.dot(hidden, weight[...], preferred_element_type=jnp.float32)
    out[...] = jnp.maximum(result + bias[...].astype(jnp.float32), 0.0).astype(out.dtype)


def local(features, adjacency, tile_column, weight, out_bias):
    groups, permutes = plan()
    axes = ("blk", "rep")
    rows, width = features.shape
    replicas = lax.axis_size("rep")

    held = jnp.stack([lax.ppermute(features, axes, pairs) for pairs in permutes])
    blocks = lax.all_to_all(
        jnp.broadcast_to(held[None], (len(groups[0]),) + held.shape), axes, 0, 0, axis_index_groups=groups
    ).reshape(LINE, rows, width)
    vmem, smem = pl.BlockSpec(memory_space=pltpu.VMEM), pl.BlockSpec(memory_space=pltpu.SMEM)
    partial = pl.pallas_call(
        aggregate_kernel,
        out_shape=jax.ShapeDtypeStruct((replicas, rows // replicas, width), jnp.bfloat16),
        in_specs=[smem, vmem, vmem],
        out_specs=vmem,
        compiler_params=pltpu.CompilerParams(vmem_limit_bytes=8 * 2**20),
    )(tile_column.reshape(-1), adjacency.reshape(adjacency.shape[2:]), blocks)
    parts = lax.all_to_all(partial, "rep", 0, 0, axis_index_groups=[list(REDUCE_ORDER)])
    return pl.pallas_call(
        project_kernel,
        out_shape=jax.ShapeDtypeStruct((rows // replicas, width), jnp.bfloat16),
        in_specs=[vmem, vmem, vmem],
        out_specs=vmem,
        compiler_params=pltpu.CompilerParams(vmem_limit_bytes=4 * 2**20),
    )(parts, weight, out_bias.reshape(1, width))


def solution(mesh):
    in_specs = (P("blk", None), P("blk", "rep", None, None, None), P("blk", "rep", None), P(), P())
    out_specs = P(("blk", "rep"), None)
    return jax.shard_map(local, mesh=mesh, in_specs=in_specs, out_specs=out_specs, check_vma=False)
```

```python
import functools
import itertools

import jax
import jax.numpy as jnp
from jax import lax
from jax.experimental import pallas as pl
from jax.experimental.pallas import tpu as pltpu
from jax.sharding import PartitionSpec as P

SIDE, RING, LINE = 4, 16, 8
REDUCE_ORDER = 1, 0, 7, 6, 5, 4, 3, 2


def device(x, y, z, core):
    x, y, z = x % SIDE, y % SIDE, z % RING
    return ((z % LINE * SIDE + x) * 2 + core) * LINE + y * 2 + z // LINE


def user(kind, y, z):
    half = z % RING // LINE
    core = (kind + half) % 2
    return ((kind - core + half) // 2 + y) % SIDE, y, z % RING, core


def apart(one, other, size):
    return min((one - other) % size, (other - one) % size)


@functools.cache
def plan():
    groups, receivers = [], ({}, {})
    for kind in range(LINE):
        even = 1 - kind % 2
        for low, first in itertools.product(range(even, RING, 2), (even, even + 2)):
            group = []
            for z in (low, low + 1):
                pair = [user(kind, (first + i) % SIDE, z) for i in range(2)]
                group += sorted(pair, key=lambda place: apart(place[0], kind // 2, SIDE))
            groups.append([device(*place) for place in group])
            for later, at in itertools.product(range(2), range(SIDE)):
                hops = SIDE - 1 - at
                key = (low + later + (hops if later else -hops)) % RING, kind
                receivers[at % 2].setdefault(key, []).append(group[2 * later + at // 2])
    permutes = []
    for wanted in receivers:
        pairs = []
        for (z, kind), places in wanted.items():

            def cost(rows):
                hops = [
                    apart(kind // 2, place[0], SIDE) + apart(row, place[1], SIDE) + apart(z, place[2], RING)
                    for row, place in zip(rows, places)
                ]
                return max(hops), sum(hops)

            rows = min(itertools.permutations(range(SIDE)), key=cost)
            pairs += [
                (device(kind // 2, row, z, kind % 2), device(*place)) for row, place in zip(rows, places)
            ]
        permutes.append(pairs)
    return groups, permutes


def aggregate_kernel(columns, adjacency, blocks, out):
    blk, rep = lax.axis_index("blk"), lax.axis_index("rep")
    low = blk // LINE - ((blk // LINE ^ blk ^ rep ^ 1) & 1)
    slots = range(adjacency.shape[0])
    total = None
    for slot in slots:
        ahead = (columns[slot] // LINE - low + 3) & (LINE - 1)
        block = blocks[jnp.where(ahead > 3, ahead ^ 3, ahead)]
        block = jnp.where(columns[slot] >= 0, block, jnp.zeros_like(block))
        product = jnp.dot(adjacency[slot], block, preferred_element_type=jnp.float32)
        total = product if total is None else total + product

    own = out.shape[1]
    for at, replica in enumerate(REDUCE_ORDER):
        out[at] = total[replica * own : (replica + 1) * own].astype(out.dtype)


def project_kernel(parts, weight, bias, out):
    hidden = jnp.sum(parts[...].astype(jnp.float32), axis=0).astype(jnp.bfloat16)
    result = jnp.dot(hidden, weight[...], preferred_element_type=jnp.float32)
    out[...] = jnp.maximum(result + bias[...].astype(jnp.float32), 0.0).astype(out.dtype)


def local(features, adjacency, tile_column, weight, out_bias):
    groups, permutes = plan()
    axes = ("blk", "rep")
    rows, width = features.shape
    replicas = lax.axis_size("rep")

    held = jnp.stack([lax.ppermute(features, axes, pairs) for pairs in permutes])
    blocks = lax.all_to_all(
        jnp.broadcast_to(held[None], (len(groups[0]),) + held.shape), axes, 0, 0, axis_index_groups=groups
    ).reshape(LINE, rows, width)
    vmem, smem = pl.BlockSpec(memory_space=pltpu.VMEM), pl.BlockSpec(memory_space=pltpu.SMEM)
    partial = pl.pallas_call(
        aggregate_kernel,
        out_shape=jax.ShapeDtypeStruct((replicas, rows // replicas, width), jnp.bfloat16),
        in_specs=[smem, vmem, vmem],
        out_specs=vmem,
        compiler_params=pltpu.CompilerParams(vmem_limit_bytes=8 * 2**20),
    )(tile_column.reshape(-1), adjacency.reshape(adjacency.shape[2:]), blocks)
    parts = lax.all_to_all(partial, "rep", 0, 0, axis_index_groups=[list(REDUCE_ORDER)])
    return pl.pallas_call(
        project_kernel,
        out_shape=jax.ShapeDtypeStruct((rows // replicas, width), jnp.bfloat16),
        in_specs=[vmem, vmem, vmem],
        out_specs=vmem,
        compiler_params=pltpu.CompilerParams(vmem_limit_bytes=4 * 2**20),
    )(parts, weight, out_bias.reshape(1, width))


def solution(mesh):
    in_specs = (P("blk", None), P("blk", "rep", None, None, None), P("blk", "rep", None), P(), P())
    out_specs = P(("blk", "rep"), None)
    return jax.shard_map(local, mesh=mesh, in_specs=in_specs, out_specs=out_specs, check_vma=False)
```
